32 devices in a mesh: dp: 16 (over z, y, x), tensor: 2 (over core).
Axes of the slice: x: 2, y: 2, z: 4, core: 2. Of those that a mesh axis runs over, the one named last changes fastest.
Arguments:
- inputs: bfloat16 [32768, 768], P(('dp', 'tensor')), may hold values from -6 to 6
- out_grad: bfloat16 [32768, 768], P(('dp', 'tensor')), may hold values from -6 to 6
- lengths: int32 [16], P('dp'), may hold values from 1025 to 2048
- w_qkv: bfloat16 [3, 768, 768], P(None, 'dp', 'tensor'), may hold values from -0.21875 to 0.21875
- w_out: bfloat16 [768, 768], P('tensor', 'dp'), may hold values from -1.75 to 1.75
- w_up: bfloat16 [768, 3072], P('dp', 'tensor'), may hold values from -0.21875 to 0.21875
- w_down: bfloat16 [3072, 768], P('tensor', 'dp'), may hold values from -0.109375 to 0.109375
- gains: bfloat16 [2, 768], replicated, may hold values from 0.099609375 to 1.8984375
- shifts: bfloat16 [4, 768], replicated, may hold values from -3 to 3
- ff_bias: bfloat16 [3072], P('tensor'), may hold values from -3 to 3
Outputs:
- out: bfloat16 [32768, 768], P(('dp', 'tensor'))
- grad_inputs: float32 [32768, 768], P(('dp', 'tensor'))
- grad_qkv: float32 [3, 768, 768], P(None, 'dp', 'tensor')
- grad_out_proj: float32 [768, 768], P('tensor', 'dp')
- grad_up: float32 [768, 3072], P('dp', 'tensor')
- grad_down: float32 [3072, 768], P('tensor', 'dp')
- grad_gains: float32 [2, 768], replicated
- grad_shifts: float32 [4, 768], replicated
- grad_ff_bias: float32 [3072], P('tensor')
The draws below stay inside these ranges and needn't reach their ends.
All inputs are finite; a program needn't handle non-finite values.
Results may differ from the reference program's by a relative error of at most 0.015.
The reference program's roundings to bfloat16 on the way count: a program that leaves them out, or rounds other values in their place, can miss the bound.
Values may be sent and summed in bfloat16 or wider, within the bound.
A program may use at most 192 MiB of HBM per device.

```python
from functools import partial
import jax
import jax.numpy as jnp
from jax import lax

D = 768
HEADS = 12
HD = 64
FF = 3072
LEN = 2048
HH = 768
SEQS = 16
TOKENS = 32768


def plant(values, stream_key, low, top_value):
    extent = values.shape
    spot = [jax.random.randint(jax.random.fold_in(stream_key, axis), (), 0, extent[axis]) for axis in range(len(extent))]
    values = values.at[tuple(spot)].set(low)
    longest = extent.index(max(extent))
    spot[longest] = (spot[longest] + 1) % extent[longest]
    return values.at[tuple(spot)].set(top_value)


def strengthened(array, stream_key, source, target, shards_of, factor):
    owner, partner = [(jnp.arange(array.shape[axis_at]) // (array.shape[axis_at] // shards_of)).reshape([-1 if axis == axis_at else 1 for axis in range(array.ndim)]) for axis_at in (source, target)]
    chosen = jax.random.permutation(stream_key, shards_of)[partner]
    strong = (owner == chosen) | (owner == (partner + shards_of // 2) % shards_of)
    return jnp.where(strong, factor * array, array)


def level_of(key, shape, shards, low, high):
    def one(dim, shards_of):
        heights = jax.random.uniform(jax.random.fold_in(jax.random.fold_in(key, 6), dim), (shards_of,), jnp.float32, low / len(shards), high / len(shards))
        return jnp.repeat(jnp.exp(heights), shape[dim] // shards_of).reshape((-1,) + (1,) * (len(shape) - dim - 1))

    loudness = one(*shards[0])
    for cut in shards[1:]:
        loudness = loudness * one(*cut)
    return loudness


def noise(stream_key, shape, deviation, bound, shards=(), kind=jnp.bfloat16):
    factor_of = level_of(stream_key, shape, shards, -0.22, 0.18) if shards else 1.0
    values = jax.random.normal(stream_key, shape, jnp.float32) * deviation * factor_of
    return jnp.minimum(jnp.maximum(values, -bound), bound).astype(kind)


def noise_with(rng, extent, deviation, most, pieces, heavy, held_as=jnp.bfloat16):
    values = deviation * jax.random.normal(rng, extent, jnp.float32)
    if pieces:
        values = values * level_of(rng, extent, pieces, -0.22, 0.18)
    return jnp.clip(strengthened(values, jax.random.fold_in(rng, 3), *heavy), -most, most).astype(held_as)


def setup_inputs(seed: int = 0) -> dict:
    seeds = jax.random.split(jax.random.key(seed), 11)
    inputs = noise(seeds[0], (TOKENS, D), 1.0, 6.0, ((0, 32),))
    out_grad = noise_with(seeds[1], (TOKENS, D), 1.0, 6.0, ((0, 32),), (0, 1, 32, 2.75))
    lengths = plant(jax.random.randint(seeds[2], (SEQS,), LEN // 2 + 1, LEN + 1), jax.random.fold_in(seeds[2], 1), LEN // 2 + 1, LEN).astype(jnp.int32)
    w_qkv = noise(seeds[3], (3, D, HH), D ** -0.5, 0.21875, ((1, 16), (2, 2)))
    w_out = noise(seeds[4], (HH, D), (HH * 32 // LEN) ** -0.5, 1.75, ((0, 2), (1, 16)))
    w_up = noise(seeds[5], (D, FF), D ** -0.5, 0.21875, ((0, 16), (1, 2)))
    w_down = noise(seeds[6], (FF, D), FF ** -0.5, 0.109375, ((0, 2), (1, 16)))
    gains = jnp.clip(1.0 + 0.18 * jax.random.normal(seeds[7], (2, D), jnp.float32), 0.099609375, 1.8984375).astype(jnp.bfloat16)
    shifts = noise(seeds[8], (4, D), 0.5, 3.0)
    ff_bias = noise(seeds[9], (FF,), 0.5, 3.0, ((0, 2),))
    return {"inputs": inputs, "out_grad": out_grad, "lengths": lengths, "w_qkv": w_qkv, "w_out": w_out, "w_up": w_up, "w_down": w_down, "gains": gains, "shifts": shifts, "ff_bias": ff_bias}


norm_eps = 1e-06

@jax.custom_vjp
def low(v):
    return lax.optimization_barrier(v.astype(jnp.bfloat16)).astype(jnp.float32)

@jax.custom_vjp
def low_back(v):
    return v

def low_keep(v):
    return (low(v), None)

def low_pass(kept, grad):
    return (grad,)

def back_keep(v):
    return (v, None)

def back_low(kept, grad):
    return (low(grad),)
low.defvjp(low_keep, low_pass)
low_back.defvjp(back_keep, back_low)

def layer_norm(hidden, gain, shift):
    center = hidden - lax.optimization_barrier(jnp.mean(hidden, axis=-1, keepdims=True))
    spread = lax.optimization_barrier(jnp.mean(center * center, axis=-1, keepdims=True))
    return center * lax.rsqrt(spread + norm_eps) * gain + shift

def attend_seq(packed):
    queries, keys_in, values_in, seq_len = packed
    highest = lax.Precision.HIGHEST
    scores = jnp.einsum('qhd,khd->hqk', queries, keys_in, precision=highest)
    scores = low_back(scores)
    key_mask = jnp.arange(LEN, dtype=jnp.int32) < seq_len
    scores = jnp.where(key_mask[None, None, :], scores, -1e+30)
    row_max = lax.optimization_barrier(jnp.max(scores, axis=-1, keepdims=True))
    shifted = jnp.exp(scores - row_max)
    attn_probs = low(shifted / lax.optimization_barrier(jnp.sum(shifted, axis=-1, keepdims=True)))
    return jnp.einsum('hqk,khd->qhd', attn_probs, values_in, precision=highest)

def forward(lengths, inputs, w_qkv, w_out, w_up, w_down, gains, shifts, ff_bias):
    highest = lax.Precision.HIGHEST
    score_scale = HD ** (-0.5)
    queries = low(low_back(jnp.dot(inputs, w_qkv[0], precision=highest) * score_scale))
    keys_all = low(low_back(jnp.dot(inputs, w_qkv[1], precision=highest)))
    values_all = low(low_back(jnp.dot(inputs, w_qkv[2], precision=highest)))
    shape_four = (SEQS, LEN, HEADS, HD)
    context = lax.map(jax.checkpoint(attend_seq), (queries.reshape(shape_four), keys_all.reshape(shape_four), values_all.reshape(shape_four), lengths))
    context = low(low_back(context.reshape(TOKENS, HH)))
    attn_branch = low_back(jnp.dot(context, w_out, precision=highest) + shifts[0])
    resid_one = inputs + attn_branch
    normed_one = low(layer_norm(resid_one, gains[0], shifts[1]))
    ff_pre = low_back(jnp.dot(normed_one, w_up, precision=highest) + ff_bias)
    ff_act = low(jax.nn.gelu(ff_pre, approximate=False))
    mlp_branch = low_back(jnp.dot(ff_act, w_down, precision=highest) + shifts[2])
    return layer_norm(normed_one + mlp_branch, gains[1], shifts[3])

def reference(inputs, out_grad, lengths, w_qkv, w_out, w_up, w_down, gains, shifts, ff_bias):
    floats = jax.tree.map(lambda matrix: matrix.astype(jnp.float32), (inputs, w_qkv, w_out, w_up, w_down, gains, shifts, ff_bias))
    result, pull_back = jax.vjp(partial(forward, lengths), *floats)
    grads = pull_back(out_grad.astype(jnp.float32))
    return (result.astype(jnp.bfloat16), grads[0], grads[1], grads[2], grads[3], grads[4], grads[5], grads[6], grads[7])
```

```python
import jax
import jax.numpy as jnp
from jax import lax
from jax.experimental import pallas as pl
from jax.experimental.pallas import tpu as pltpu
from jax.sharding import PartitionSpec as P

HD = 64
LEN = 2048


norm_eps = 1e-06
masked_score = -1e30


def layer_norm(hidden, gain, shift):
    center = hidden - jnp.mean(hidden, axis=-1, keepdims=True)
    spread = jnp.mean(center * center, axis=-1, keepdims=True)
    return center * lax.rsqrt(spread + norm_eps) * gain + shift


def exact_gelu(ff_pre):
    return jax.nn.gelu(ff_pre, approximate=False)


PAIR = 2 * HD
QUERY_ROWS = 512
KEY_ROWS = 512


def split_heads(rows):
    lane = lax.broadcasted_iota(jnp.int32, rows.shape, 1)
    blank = jnp.zeros_like(rows)
    return (jnp.where(lane < HD, rows, blank), jnp.where(lane < HD, blank, rows))


def dot_nt(left, right):
    return lax.dot_general(
        left, right, (((1,), (1,)), ((), ())), preferred_element_type=jnp.float32
    )


def dot_nn(left, right):
    return jnp.dot(left, right, preferred_element_type=jnp.float32)


def masked_scores(key_block, query_head, chunk, seq_len):
    scores = dot_nt(key_block, query_head)
    if (chunk + 1) * KEY_ROWS > LEN // 2:
        place = lax.broadcasted_iota(jnp.int32, scores.shape, 0) + chunk * KEY_ROWS
        scores = jnp.where(place < seq_len, scores, masked_score)
    return scores


def forward_kernel(lens_ref, q_ref, k_ref, vt_ref, ctx_ref, lse_ref):
    seq_len = lens_ref[pl.program_id(0)]
    parts = []
    for head, query_head in enumerate(split_heads(q_ref[...])):
        rows = pl.ds(head * HD, HD)
        blocks = [
            masked_scores(k_ref[pl.ds(c * KEY_ROWS, KEY_ROWS), :], query_head, c, seq_len)
            for c in range(LEN // KEY_ROWS)
        ]
        tops = [jnp.max(block, axis=0, keepdims=True) for block in blocks]
        top = tops[0]
        for other in tops[1:]:
            top = jnp.maximum(top, other)
        total = jnp.zeros_like(top)
        context = jnp.zeros((HD, QUERY_ROWS), jnp.float32)
        for c, block in enumerate(blocks):
            shifted = jnp.exp(block - top)
            total = total + jnp.sum(shifted, axis=0, keepdims=True)
            context = context + dot_nn(
                vt_ref[rows, pl.ds(c * KEY_ROWS, KEY_ROWS)], shifted.astype(jnp.bfloat16)
            )
        parts.append(context / total)
        lse_ref[0, 0, pl.ds(head, 1), :] = top + jnp.log(total)
    ctx_ref[...] = jnp.concatenate(parts, axis=0).T.astype(jnp.bfloat16)


def backward_kernel(
    lens_ref, q_ref, k_ref, kt_ref, v_ref, ctx_ref, grad_ref, lse_ref,
    dq_ref, dk_ref, dv_ref, key_sum, value_sum,
):
    seq_len = lens_ref[pl.program_id(0)]
    step = pl.program_id(2)

    @pl.when(step == 0)
    def _():
        key_sum[...] = jnp.zeros_like(key_sum)
        value_sum[...] = jnp.zeros_like(value_sum)

    product = (grad_ref[...].astype(jnp.float32) * ctx_ref[...].astype(jnp.float32)).T
    deltas = [
        jnp.sum(product[h * HD : (h + 1) * HD], axis=0, keepdims=True) for h in range(2)
    ]
    query_heads = split_heads(q_ref[...])
    grad_heads = split_heads(grad_ref[...])
    query_grads = [jnp.zeros((HD, QUERY_ROWS), jnp.float32) for _ in range(2)]
    for c in range(LEN // KEY_ROWS):
        span = pl.ds(c * KEY_ROWS, KEY_ROWS)
        key_add = None
        value_add = None
        for head in range(2):
            scores = masked_scores(k_ref[span, :], query_heads[head], c, seq_len)
            probs = jnp.exp(scores - lse_ref[0, 0, pl.ds(head, 1), :])
            prob_grad = dot_nt(v_ref[span, :], grad_heads[head])
            score_grad = (probs * (prob_grad - deltas[head])).astype(jnp.bfloat16)
            value_part = dot_nn(probs.astype(jnp.bfloat16), grad_heads[head])
            key_part = dot_nn(score_grad, query_heads[head])
            value_add = value_part if head == 0 else value_add + value_part
            key_add = key_part if head == 0 else key_add + key_part
            query_grads[head] = query_grads[head] + dot_nn(
                kt_ref[pl.ds(head * HD, HD), span], score_grad
            )
        key_sum[span, :] += key_add
        value_sum[span, :] += value_add
    query_grad = jnp.concatenate(query_grads, axis=0).T.astype(jnp.bfloat16)
    dq_ref[...] = (query_grad.astype(jnp.float32) * HD ** (-0.5)).astype(jnp.bfloat16)

    @pl.when(step == pl.num_programs(2) - 1)
    def _():
        dk_ref[...] = key_sum[...].astype(jnp.bfloat16)
        dv_ref[...] = value_sum[...].astype(jnp.bfloat16)


def attention_specs():
    blocks = LEN // QUERY_ROWS
    lens = pl.BlockSpec(memory_space=pltpu.SMEM)
    query = pl.BlockSpec((QUERY_ROWS, PAIR), lambda s, p, i: (s * blocks + i, p))
    whole = pl.BlockSpec((LEN, PAIR), lambda s, p, i: (s, p))
    turned = pl.BlockSpec((PAIR, LEN), lambda s, p, i: (p, s))
    lse = pl.BlockSpec((1, 1, 2, QUERY_ROWS), lambda s, p, i: (s, p, 0, i))
    return lens, query, whole, turned, lse


def attend(lengths, queries, keys_all, values_turned):
    seqs, pairs = lengths.shape[0], queries.shape[1] // PAIR
    lens, query, whole, turned, lse = attention_specs()
    return pl.pallas_call(
        forward_kernel,
        grid=(seqs, pairs, LEN // QUERY_ROWS),
        in_specs=[lens, query, whole, turned],
        out_specs=[query, lse],
        out_shape=[
            jax.ShapeDtypeStruct(queries.shape, jnp.bfloat16),
            jax.ShapeDtypeStruct((seqs, pairs, 2, LEN), jnp.float32),
        ],
        compiler_params=pltpu.CompilerParams(vmem_limit_bytes=56 * 1024 * 1024),
        name="attend_forward",
    )(lengths, queries, keys_all, values_turned)


def attend_back(lengths, queries, keys_all, keys_turned, values_all, context, context_grad, stats):
    seqs, pairs = lengths.shape[0], queries.shape[1] // PAIR
    lens, query, whole, turned, lse = attention_specs()
    shape = jax.ShapeDtypeStruct(queries.shape, jnp.bfloat16)
    return pl.pallas_call(
        backward_kernel,
        grid=(seqs, pairs, LEN // QUERY_ROWS),
        in_specs=[lens, query, whole, turned, whole, query, query, lse],
        out_specs=[query, whole, whole],
        out_shape=[shape, shape, shape],
        scratch_shapes=[pltpu.VMEM((LEN, PAIR), jnp.float32)] * 2,
        compiler_params=pltpu.CompilerParams(vmem_limit_bytes=56 * 1024 * 1024),
        name="attend_backward",
    )(lengths, queries, keys_all, keys_turned, values_all, context, context_grad, stats)


def owned_parts(*grads):
    count = lax.axis_size("dp")
    pieces, shapes = [], []
    for grad, dim in grads:
        cut = grad.shape[:dim] + (count, grad.shape[dim] // count) + grad.shape[dim + 1 :]
        piece = jnp.moveaxis(grad.astype(jnp.bfloat16).reshape(cut), dim, 0)
        shapes.append(piece.shape[1:])
        pieces.append(piece.reshape(count, -1, 128))
    sent = lax.all_to_all(
        jnp.concatenate(pieces, axis=1), "dp", split_axis=0, concat_axis=0, tiled=True
    )
    summed = jnp.sum(sent.astype(jnp.float32), axis=0)
    owned, start = [], 0
    for piece, shape in zip(pieces, shapes):
        owned.append(summed[start : start + piece.shape[1]].reshape(shape))
        start += piece.shape[1]
    return owned


def body(inputs, out_grad, lengths, w_qkv, w_out, w_up, w_down, gains, shifts, ff_bias):
    score_scale = HD ** (-0.5)
    seq_count = lengths.shape[0]
    head_count = w_qkv.shape[2] // HD
    gains_f = gains.astype(jnp.float32)
    shifts_f = shifts.astype(jnp.float32)
    inputs_f = inputs.astype(jnp.float32)
    gathered = lax.all_gather(inputs, "tensor", axis=0, tiled=True)
    qkv_full, out_full = (
        lax.all_gather(w_qkv, "dp", axis=1, tiled=True),
        lax.all_gather(w_out, "dp", axis=1, tiled=True),
    )
    projected = jnp.einsum("rd,cde->cre", gathered, qkv_full, preferred_element_type=jnp.float32)
    queries = (projected[0] * score_scale).astype(jnp.bfloat16)
    keys_all = projected[1].astype(jnp.bfloat16)
    values_all = projected[2].astype(jnp.bfloat16)
    context, stats = attend(lengths, queries, keys_all, values_all.T)
    attn_branch = (
        lax.psum_scatter(
            jnp.dot(context, out_full, preferred_element_type=jnp.float32),
            "tensor",
            scatter_dimension=0,
            tiled=True,
        )
        + shifts_f[0]
    )
    resid_one = inputs_f + attn_branch
    normed_f, norm_one_back = jax.vjp(layer_norm, resid_one, gains_f[0], shifts_f[1])
    normed_one = normed_f.astype(jnp.bfloat16)
    normed_all = lax.all_gather(normed_one, "tensor", axis=0, tiled=True)
    up_full, down_full = (
        lax.all_gather(w_up, "dp", axis=0, tiled=True),
        lax.all_gather(w_down, "dp", axis=1, tiled=True),
    )
    ff_pre = jnp.dot(normed_all, up_full, preferred_element_type=jnp.float32) + ff_bias.astype(
        jnp.float32
    )
    ff_act_f, gelu_back = jax.vjp(exact_gelu, ff_pre)
    ff_act = ff_act_f.astype(jnp.bfloat16)
    mlp_branch = (
        lax.psum_scatter(
            jnp.dot(ff_act, down_full, preferred_element_type=jnp.float32),
            "tensor",
            scatter_dimension=0,
            tiled=True,
        )
        + shifts_f[2]
    )
    resid_two = normed_one.astype(jnp.float32) + mlp_branch
    result, norm_two_back = jax.vjp(layer_norm, resid_two, gains_f[1], shifts_f[3])
    resid_two_grad, gain_two_grad, shift_three_grad = norm_two_back(out_grad.astype(jnp.float32))
    mlp_grad = resid_two_grad.astype(jnp.bfloat16)
    shift_two_grad = jnp.sum(mlp_grad.astype(jnp.float32), axis=0)
    mlp_grad_all = lax.all_gather(mlp_grad, "tensor", axis=0, tiled=True)
    act_grad = jnp.einsum("rd,fd->rf", mlp_grad_all, down_full, preferred_element_type=jnp.float32)
    down_grad = jnp.einsum("rf,rd->fd", ff_act, mlp_grad_all, preferred_element_type=jnp.float32)
    pre_grad = gelu_back(act_grad)[0].astype(jnp.bfloat16)
    bias_grad = jnp.sum(pre_grad.astype(jnp.float32), axis=0)
    up_grad = jnp.einsum("rd,rf->df", normed_all, pre_grad, preferred_element_type=jnp.float32)
    slab_rows = pre_grad
    normed_grad = resid_two_grad + lax.psum_scatter(
        jnp.einsum("rf,df->rd", slab_rows, up_full, preferred_element_type=jnp.float32),
        "tensor",
        scatter_dimension=0,
        tiled=True,
    )
    resid_one_grad, gain_one_grad, shift_one_grad = norm_one_back(normed_grad)
    attn_grad = resid_one_grad.astype(jnp.bfloat16)
    shift_zero_grad = jnp.sum(attn_grad.astype(jnp.float32), axis=0)
    attn_grad_all = lax.all_gather(attn_grad, "tensor", axis=0, tiled=True)
    context_grad = jnp.einsum(
        "rd,ed->re", attn_grad_all, out_full, preferred_element_type=jnp.float32
    ).astype(jnp.bfloat16)
    out_proj_grad = jnp.einsum(
        "re,rd->ed", context, attn_grad_all, preferred_element_type=jnp.float32
    )
    down_owned, up_owned, out_owned = owned_parts(
        (down_grad, 1), (up_grad, 0), (out_proj_grad, 1)
    )
    stacked_grad = jnp.stack(
        attend_back(
            lengths, queries, keys_all, keys_all.T, values_all, context, context_grad, stats
        )
    )
    qkv_grad = jnp.einsum("rd,cre->cde", gathered, stacked_grad, preferred_element_type=jnp.float32)
    (qkv_owned,) = owned_parts((qkv_grad, 1))
    slab_rows = stacked_grad
    parts = jnp.einsum("cre,cde->rd", slab_rows, qkv_full, preferred_element_type=jnp.float32)
    input_grad = resid_one_grad + lax.psum_scatter(
        parts.astype(jnp.bfloat16),
        "tensor",
        scatter_dimension=0,
        tiled=True,
    ).astype(jnp.float32)
    gain_grads = jnp.stack([gain_one_grad, gain_two_grad])
    shift_grads = jnp.stack([shift_zero_grad, shift_one_grad, shift_two_grad, shift_three_grad])
    tensor_count = lax.axis_size("tensor")
    own_slot = (jnp.arange(tensor_count, dtype=jnp.int32) == lax.axis_index("tensor")).astype(
        jnp.float32
    )
    spread_bias = own_slot[:, None] * bias_grad[None, :]
    gain_sum, shift_sum, bias_sum = lax.psum(
        (gain_grads, shift_grads, spread_bias), ("dp", "tensor")
    )
    bias_owned = jnp.sum(own_slot[:, None] * bias_sum, axis=0)
    return (
        result.astype(jnp.bfloat16),
        input_grad,
        qkv_owned,
        out_owned,
        up_owned,
        down_owned,
        gain_sum,
        shift_sum,
        bias_owned,
    )


def solution(mesh):
    return jax.shard_map(
        body,
        mesh=mesh,
        in_specs=(
            P(("dp", "tensor"), None),
            P(("dp", "tensor"), None),
            P("dp"),
            P(None, "dp", "tensor"),
            P("tensor", "dp"),
            P("dp", "tensor"),
            P("tensor", "dp"),
            P(),
            P(),
            P("tensor"),
        ),
        out_specs=(
            P(("dp", "tensor"), None),
            P(("dp", "tensor"), None),
            P(None, "dp", "tensor"),
            P("tensor", "dp"),
            P("dp", "tensor"),
            P("tensor", "dp"),
            P(),
            P(),
            P("tensor"),
        ),
        check_vma=False,
    )
```

```python
import jax
import jax.numpy as jnp
from jax import lax
from jax.experimental import pallas as pl
from jax.experimental.pallas import tpu as pltpu
from jax.sharding import PartitionSpec as P

HD = 64
LEN = 2048


norm_eps = 1e-06
masked_score = -1e30


def layer_norm(hidden, gain, shift):
    center = hidden - jnp.mean(hidden, axis=-1, keepdims=True)
    spread = jnp.mean(center * center, axis=-1, keepdims=True)
    return center * lax.rsqrt(spread + norm_eps) * gain + shift


def exact_gelu(ff_pre):
    return jax.nn.gelu(ff_pre, approximate=False)


PAIR = 2 * HD
QUERY_ROWS = 512
KEY_ROWS = 512


def split_heads(rows):
    lane = lax.broadcasted_iota(jnp.int32, rows.shape, 1)
    blank = jnp.zeros_like(rows)
    return (jnp.where(lane < HD, rows, blank), jnp.where(lane < HD, blank, rows))


def dot_nt(left, right):
    return lax.dot_general(
        left, right, (((1,), (1,)), ((), ())), preferred_element_type=jnp.float32
    )


def dot_nn(left, right):
    return jnp.dot(left, right, preferred_element_type=jnp.float32)


def masked_scores(key_block, query_head, chunk, seq_len):
    scores = dot_nt(key_block, query_head)
    if (chunk + 1) * KEY_ROWS > LEN // 2:
        place = lax.broadcasted_iota(jnp.int32, scores.shape, 0) + chunk * KEY_ROWS
        scores = jnp.where(place < seq_len, scores, masked_score)
    return scores


def forward_kernel(lens_ref, q_ref, k_ref, vt_ref, ctx_ref, lse_ref):
    seq_len = lens_ref[pl.program_id(0)]
    parts = []
    for head, query_head in enumerate(split_heads(q_ref[...])):
        rows = pl.ds(head * HD, HD)
        blocks = [
            masked_scores(k_ref[pl.ds(c * KEY_ROWS, KEY_ROWS), :], query_head, c, seq_len)
            for c in range(LEN // KEY_ROWS)
        ]
        tops = [jnp.max(block, axis=0, keepdims=True) for block in blocks]
        top = tops[0]
        for other in tops[1:]:
            top = jnp.maximum(top, other)
        total = jnp.zeros_like(top)
        context = jnp.zeros((HD, QUERY_ROWS), jnp.float32)
        for c, block in enumerate(blocks):
            shifted = jnp.exp(block - top)
            total = total + jnp.sum(shifted, axis=0, keepdims=True)
            context = context + dot_nn(
                vt_ref[rows, pl.ds(c * KEY_ROWS, KEY_ROWS)], shifted.astype(jnp.bfloat16)
            )
        parts.append(context / total)
        lse_ref[0, 0, pl.ds(head, 1), :] = top + jnp.log(total)
    ctx_ref[...] = jnp.concatenate(parts, axis=0).T.astype(jnp.bfloat16)


def backward_kernel(
    lens_ref, q_ref, k_ref, kt_ref, v_ref, ctx_ref, grad_ref, lse_ref,
    dq_ref, dk_ref, dv_ref, key_sum, value_sum,
):
    seq_len = lens_ref[pl.program_id(0)]
    step = pl.program_id(2)

    @pl.when(step == 0)
    def _():
        key_sum[...] = jnp.zeros_like(key_sum)
        value_sum[...] = jnp.zeros_like(value_sum)

    product = (grad_ref[...].astype(jnp.float32) * ctx_ref[...].astype(jnp.float32)).T
    deltas = [
        jnp.sum(product[h * HD : (h + 1) * HD], axis=0, keepdims=True) for h in range(2)
    ]
    query_heads = split_heads(q_ref[...])
    grad_heads = split_heads(grad_ref[...])
    query_grads = [jnp.zeros((HD, QUERY_ROWS), jnp.float32) for _ in range(2)]
    for c in range(LEN // KEY_ROWS):
        span = pl.ds(c * KEY_ROWS, KEY_ROWS)
        key_add = None
        value_add = None
        for head in range(2):
            scores = masked_scores(k_ref[span, :], query_heads[head], c, seq_len)
            probs = jnp.exp(scores - lse_ref[0, 0, pl.ds(head, 1), :])
            prob_grad = dot_nt(v_ref[span, :], grad_heads[head])
            score_grad = (probs * (prob_grad - deltas[head])).astype(jnp.bfloat16)
            value_part = dot_nn(probs.astype(jnp.bfloat16), grad_heads[head])
            key_part = dot_nn(score_grad, query_heads[head])
            value_add = value_part if head == 0 else value_add + value_part
            key_add = key_part if head == 0 else key_add + key_part
            query_grads[head] = query_grads[head] + dot_nn(
                kt_ref[pl.ds(head * HD, HD), span], score_grad
            )
        key_sum[span, :] += key_add
        value_sum[span, :] += value_add
    query_grad = jnp.concatenate(query_grads, axis=0).T.astype(jnp.bfloat16)
    dq_ref[...] = (query_grad.astype(jnp.float32) * HD ** (-0.5)).astype(jnp.bfloat16)

    @pl.when(step == pl.num_programs(2) - 1)
    def _():
        dk_ref[...] = key_sum[...].astype(jnp.bfloat16)
        dv_ref[...] = value_sum[...].astype(jnp.bfloat16)


def attention_specs():
    blocks = LEN // QUERY_ROWS
    lens = pl.BlockSpec(memory_space=pltpu.SMEM)
    query = pl.BlockSpec((QUERY_ROWS, PAIR), lambda s, p, i: (s * blocks + i, p))
    whole = pl.BlockSpec((LEN, PAIR), lambda s, p, i: (s, p))
    turned = pl.BlockSpec((PAIR, LEN), lambda s, p, i: (p, s))
    lse = pl.BlockSpec((1, 1, 2, QUERY_ROWS), lambda s, p, i: (s, p, 0, i))
    return lens, query, whole, turned, lse


def attend(lengths, queries, keys_all, values_turned):
    seqs, pairs = lengths.shape[0], queries.shape[1] // PAIR
    lens, query, whole, turned, lse = attention_specs()
    return pl.pallas_call(
        forward_kernel,
        grid=(seqs, pairs, LEN // QUERY_ROWS),
        in_specs=[lens, query, whole, turned],
        out_specs=[query, lse],
        out_shape=[
            jax.ShapeDtypeStruct(queries.shape, jnp.bfloat16),
            jax.ShapeDtypeStruct((seqs, pairs, 2, LEN), jnp.float32),
        ],
        compiler_params=pltpu.CompilerParams(vmem_limit_bytes=56 * 1024 * 1024),
        cost_estimate=pl.CostEstimate(
            flops=seqs * pairs * 16 * LEN * LEN * PAIR,
            transcendentals=seqs * pairs * 2 * LEN * LEN,
            bytes_accessed=8 * queries.size,
        ),
        name="attend_forward",
    )(lengths, queries, keys_all, values_turned)


def attend_back(lengths, queries, keys_all, keys_turned, values_all, context, context_grad, stats):
    seqs, pairs = lengths.shape[0], queries.shape[1] // PAIR
    lens, query, whole, turned, lse = attention_specs()
    shape = jax.ShapeDtypeStruct(queries.shape, jnp.bfloat16)
    return pl.pallas_call(
        backward_kernel,
        grid=(seqs, pairs, LEN // QUERY_ROWS),
        in_specs=[lens, query, whole, turned, whole, query, query, lse],
        out_specs=[query, whole, whole],
        out_shape=[shape, shape, shape],
        scratch_shapes=[pltpu.VMEM((LEN, PAIR), jnp.float32)] * 2,
        compiler_params=pltpu.CompilerParams(vmem_limit_bytes=56 * 1024 * 1024),
        cost_estimate=pl.CostEstimate(
            flops=seqs * pairs * 28 * LEN * LEN * PAIR,
            transcendentals=seqs * pairs * 2 * LEN * LEN,
            bytes_accessed=18 * queries.size,
        ),
        name="attend_backward",
    )(lengths, queries, keys_all, keys_turned, values_all, context, context_grad, stats)


def send_blocks(blocks, axes):
    return lax.all_to_all(blocks, axes, split_axis=0, concat_axis=0, tiled=True)


def gather_rows(rows):
    count = lax.axis_size("dp")
    blocks = jnp.broadcast_to(rows[None], (count,) + rows.shape)
    return send_blocks(blocks, "dp").reshape(count * rows.shape[0], rows.shape[1])


def send_rows(rows):
    count = lax.axis_size("dp")
    return send_blocks(rows.reshape(count, rows.shape[0] // count, rows.shape[1]), "dp")


def summed(sent):
    return jnp.sum(sent.astype(jnp.float32), axis=0)


def dot_tn(left, right):
    return lax.dot_general(
        left, right, (((0,), (0,)), ((), ())), preferred_element_type=jnp.float32
    )


def body(inputs, out_grad, lengths, w_qkv, w_out, w_up, w_down, gains, shifts, ff_bias):
    score_scale = HD ** (-0.5)
    gains_f = gains.astype(jnp.float32)
    shifts_f = shifts.astype(jnp.float32)
    inputs_f = inputs.astype(jnp.float32)
    gathered = lax.all_gather(inputs, "tensor", axis=0, tiled=True)
    width = w_qkv.shape[2]
    own_first = jnp.concatenate([w_qkv[0], w_qkv[1], w_qkv[2], w_out.T], axis=1)
    first = gather_rows(own_first)
    own_up, first = lax.optimization_barrier((w_up, first))
    up_full = gather_rows(own_up)
    qkv_full, out_turned = first[:, : 3 * width], first[:, 3 * width :]
    projected = dot_nn(gathered, qkv_full)
    queries = (projected[:, :width] * score_scale).astype(jnp.bfloat16)
    keys_all = projected[:, width : 2 * width].astype(jnp.bfloat16)
    values_all = projected[:, 2 * width :].astype(jnp.bfloat16)
    context, stats = attend(lengths, queries, keys_all, values_all.T)
    own_down, up_full, context = lax.optimization_barrier((w_down.T, up_full, context))
    down_turned = gather_rows(own_down)
    attn_branch = (
        lax.psum_scatter(
            dot_nt(context, out_turned),
            "tensor",
            scatter_dimension=0,
            tiled=True,
        )
        + shifts_f[0]
    )
    resid_one = inputs_f + attn_branch
    normed_f, norm_one_back = jax.vjp(layer_norm, resid_one, gains_f[0], shifts_f[1])
    normed_one = normed_f.astype(jnp.bfloat16)
    normed_all = lax.all_gather(normed_one, "tensor", axis=0, tiled=True)
    ff_pre = jnp.dot(normed_all, up_full, preferred_element_type=jnp.float32) + ff_bias.astype(
        jnp.float32
    )
    ff_act_f, gelu_back = jax.vjp(exact_gelu, ff_pre)
    ff_act = ff_act_f.astype(jnp.bfloat16)
    mlp_branch = (
        lax.psum_scatter(
            dot_nt(ff_act, down_turned),
            "tensor",
            scatter_dimension=0,
            tiled=True,
        )
        + shifts_f[2]
    )
    resid_two = normed_one.astype(jnp.float32) + mlp_branch
    result, norm_two_back = jax.vjp(layer_norm, resid_two, gains_f[1], shifts_f[3])
    resid_two_grad, gain_two_grad, shift_three_grad = norm_two_back(out_grad.astype(jnp.float32))
    mlp_grad = resid_two_grad.astype(jnp.bfloat16)
    shift_two_grad = jnp.sum(mlp_grad.astype(jnp.float32), axis=0)
    mlp_grad_all = lax.all_gather(mlp_grad, "tensor", axis=0, tiled=True)
    down_grad = dot_tn(mlp_grad_all, ff_act).astype(jnp.bfloat16)
    down_grad, mlp_grad_all = lax.optimization_barrier((down_grad, mlp_grad_all))
    down_sent = send_rows(down_grad)
    act_grad = dot_nn(mlp_grad_all, down_turned)
    pre_grad = gelu_back(act_grad)[0].astype(jnp.bfloat16)
    bias_grad = jnp.sum(pre_grad.astype(jnp.float32), axis=0)
    up_grad = jnp.einsum("rd,rf->df", normed_all, pre_grad, preferred_element_type=jnp.float32)
    slab_rows = pre_grad
    normed_grad = resid_two_grad + lax.psum_scatter(
        jnp.einsum("rf,df->rd", slab_rows, up_full, preferred_element_type=jnp.float32),
        "tensor",
        scatter_dimension=0,
        tiled=True,
    )
    resid_one_grad, gain_one_grad, shift_one_grad = norm_one_back(normed_grad)
    attn_grad = resid_one_grad.astype(jnp.bfloat16)
    shift_zero_grad = jnp.sum(attn_grad.astype(jnp.float32), axis=0)
    attn_grad_all = lax.all_gather(attn_grad, "tensor", axis=0, tiled=True)
    context_grad = dot_nn(attn_grad_all, out_turned).astype(jnp.bfloat16)
    out_proj_grad = dot_tn(attn_grad_all, context)
    tensor_count = lax.axis_size("tensor")
    dp_count = lax.axis_size("dp")
    small = jnp.concatenate(
        [
            gain_one_grad, gain_two_grad, shift_zero_grad, shift_one_grad, shift_two_grad,
            shift_three_grad, bias_grad,
        ]
    )
    packed = jnp.concatenate(
        [up_grad.astype(jnp.bfloat16), out_proj_grad.astype(jnp.bfloat16)], axis=1
    )
    packed, small, down_sent, context_grad = lax.optimization_barrier(
        (packed, small, down_sent, context_grad)
    )
    packed_sent = send_rows(packed)
    hidden = w_up.shape[1]
    devices = dp_count * tensor_count
    small_all = send_blocks(
        jnp.broadcast_to(small[None], (devices,) + small.shape), ("dp", "tensor")
    )
    features = 6 * inputs.shape[1]
    feature_sum = jnp.sum(small_all[:, :features], axis=0).reshape(6, inputs.shape[1])
    gain_sum, shift_sum = feature_sum[:2], feature_sum[2:]
    own_slot = (jnp.arange(tensor_count, dtype=jnp.int32) == lax.axis_index("tensor")).astype(
        jnp.float32
    )
    bias_all = small_all[:, features:].reshape(dp_count, tensor_count, hidden)
    bias_owned = jnp.sum(bias_all * own_slot[None, :, None], axis=(0, 1))
    stacked_grad = attend_back(
        lengths, queries, keys_all, keys_all.T, values_all, context, context_grad, stats
    )
    packed_sent, stacked_grad = lax.optimization_barrier((packed_sent, stacked_grad))
    stacked_grad = jnp.concatenate(stacked_grad, axis=1)
    down_owned = summed(down_sent).T
    packed_owned = summed(packed_sent)
    up_owned, out_owned = packed_owned[:, :hidden], packed_owned[:, hidden:].T
    qkv_rows = summed(send_rows(dot_tn(gathered, stacked_grad).astype(jnp.bfloat16)))
    qkv_owned = qkv_rows.reshape(-1, 3, width).transpose(1, 0, 2)
    slab_rows = stacked_grad
    parts = dot_nt(slab_rows, qkv_full)
    input_grad = resid_one_grad + lax.psum_scatter(
        parts.astype(jnp.bfloat16),
        "tensor",
        scatter_dimension=0,
        tiled=True,
    ).astype(jnp.float32)
    return (
        result.astype(jnp.bfloat16),
        input_grad,
        qkv_owned,
        out_owned,
        up_owned,
        down_owned,
        gain_sum,
        shift_sum,
        bias_owned,
    )


def solution(mesh):
    return jax.shard_map(
        body,
        mesh=mesh,
        in_specs=(
            P(("dp", "tensor"), None),
            P(("dp", "tensor"), None),
            P("dp"),
            P(None, "dp", "tensor"),
            P("tensor", "dp"),
            P("dp", "tensor"),
            P("tensor", "dp"),
            P(),
            P(),
            P("tensor"),
        ),
        out_specs=(
            P(("dp", "tensor"), None),
            P(("dp", "tensor"), None),
            P(None, "dp", "tensor"),
            P("tensor", "dp"),
            P("dp", "tensor"),
            P("tensor", "dp"),
            P(),
            P(),
            P("tensor"),
        ),
        check_vma=False,
    )
```
